32 devices in a mesh: groups: 2 (over y), ffn: 4 (over z), width: 2 (over x), sub: 2 (over core).
Axes of the slice: x: 2, y: 2, z: 4, core: 2. Of those that a mesh axis runs over, the one named last changes fastest.
Arguments:
- tokens: bfloat16 [32, 16384], P(('groups', 'ffn'), ('width', 'sub')), parts along dimension 0, may hold values from -2000 to 2000
- norm_gain: bfloat16 [16384], P(('width', 'sub')), may hold values from 0.5 to 1.5
- w_qkv: bfloat16 [16384, 9216], P(('width', 'sub'), 'ffn'), may hold values from -0.046875 to 0.046875
- w_out: bfloat16 [8192, 16384], P('ffn', ('width', 'sub')), may hold values from -0.0625 to 0.0625
- kv_cache: bfloat16 [2, 32, 4096, 512], P(None, ('groups', 'width', 'sub'), 'ffn'), parts along dimension 1, may hold values from -64 to 64
- lengths: int32 [32], P(('groups', 'width', 'sub')), parts along dimension 0, may hold values from 1 to 4096, as said below
Outputs:
- attn_out: bfloat16 [32, 16384], P(('groups', 'ffn'), ('width', 'sub')), parts along dimension 0
The draws below stay inside these ranges and needn't reach their ends.
There are 2 independent parts, one for each index of `groups`. The reference program is written for one: setup_inputs(seed, part) draws one part's arguments, and reference() takes and returns one part's arrays. A program takes and returns all parts, laid end to end along the dimension named above; an argument that names none is the same for every part. Nothing has to cross between parts.
Inputs may be any that keep to these rules, and one draw needn't show every extreme that they name: lengths[r] positions of row r's cache hold data, from position 0 on; some row has exactly 4096.
All inputs are finite; a program needn't handle non-finite values.
Results may differ from the reference program's by a relative error of at most 0.012.
Values may be sent and summed in bfloat16 or wider, within the bound.
No kernel may reach another device: no remote copies, remote signals or barrier semaphores. Data moves between devices by JAX's collectives and lax.ppermute only.
A program may use at most 128 MiB of HBM per device.

```python
import math
import jax
import jax.numpy as jnp
from jax import lax

D = 16384
HQ = 64
KVH = 4
DH = 128
L = 4096
ROWS = 16
QKV = 9216


def draw_tokens(key, part):
    key = jax.random.fold_in(key, 37)
    subkeys = jax.random.split(key, 3)
    places = jnp.arange(D, dtype=jnp.float32) / (D - 1)
    sample = jnp.clip(jax.random.normal(subkeys[0], (ROWS, D), jnp.float32), -4.0, 4.0)
    row_scale = jnp.exp(jax.random.uniform(subkeys[1], (ROWS, 1), jnp.float32, 0.0, math.log(10.0)))
    column_ramp = jnp.sqrt(1.0 + 2.0 * places)
    column_scale = jnp.exp(jax.random.uniform(subkeys[2], (1, D), jnp.float32, 0.0, math.log(10.0))) * column_ramp[None, :]
    return (sample * row_scale * column_scale).astype(jnp.bfloat16)


def draw_kv_cache(key, part):
    key = jax.random.fold_in(key, 11)
    subkeys = jax.random.split(key, 1)
    full_shape = (2, ROWS, L, KVH * DH)
    scales = jnp.array([2.0, 3.0], jnp.float32).reshape(2, 1, 1, 1)
    sample = jnp.clip(jax.random.normal(subkeys[0], full_shape, jnp.float32), -8.0, 8.0) * scales
    return sample.astype(jnp.bfloat16)


def draw_lengths(key, part):
    key = jax.random.fold_in(key, 23)
    subkeys = jax.random.split(key, 2)
    filled = jax.random.randint(subkeys[0], (ROWS,), 1, L + 1)
    longest = jax.random.randint(subkeys[1], (), 0, ROWS)
    return jnp.where(jnp.arange(ROWS) == longest, L, filled).astype(jnp.int32)


def levels(stream_key, extent, pieces, low, high):
    def one(axis_at, shards_of):
        heights = jax.random.uniform(jax.random.fold_in(jax.random.fold_in(stream_key, 6), axis_at), (shards_of,), jnp.float32, low / len(pieces), high / len(pieces))
        return jnp.repeat(jnp.exp(heights), extent[axis_at] // shards_of).reshape((-1,) + (1,) * (len(extent) - axis_at - 1))

    gain = one(*pieces[0])
    for cut in pieces[1:]:
        gain = gain * one(*cut)
    return gain


def centred(own_key, dims, width, limit, cuts=(), kind=jnp.bfloat16):
    entries = width * jax.random.normal(own_key, dims, jnp.float32)
    if cuts:
        entries = entries * levels(own_key, dims, cuts, -0.22, 0.18)
    return jnp.clip(entries, -limit, limit).astype(kind)


def setup_inputs(seed: int = 0, part: int = 0) -> dict:
    key_of = jax.random.split(jax.random.key(seed), 7)
    own_keys = jax.random.split(jax.random.fold_in(key_of[6], part), 7)
    tokens = draw_tokens(jax.random.fold_in(jax.random.fold_in(key_of[6], part), 71), part)
    norm_gain = jnp.clip(0.5 + 1.0 * jax.random.uniform(key_of[1], (D,), jnp.float32) ** levels(key_of[1], (D,), ((0, 4),), -0.2, 0.2), 0.5, 1.5).astype(jnp.bfloat16)
    w_qkv = centred(key_of[2], (D, QKV), D ** -0.5, 0.046875, ((0, 4), (1, 4)))
    w_out = centred(key_of[3], (HQ * DH, D), (HQ * DH) ** -0.5, 0.0625, ((0, 4), (1, 4)))
    kv_cache = draw_kv_cache(jax.random.fold_in(jax.random.fold_in(key_of[6], part), 71), part)
    lengths = draw_lengths(jax.random.fold_in(jax.random.fold_in(key_of[6], part), 71), part)
    return {"tokens": tokens, "norm_gain": norm_gain, "w_qkv": w_qkv, "w_out": w_out, "kv_cache": kv_cache, "lengths": lengths}


def rotate(values, positions):
    half_dim = DH // 2
    frequency = 500000.0 ** (-(jnp.arange(half_dim, dtype=jnp.float32) * 2.0 / DH))
    angles = positions * frequency
    cosine = jnp.cos(angles)
    sine_part = jnp.sin(angles)
    first_half = values[..., :half_dim]
    second_half = values[..., half_dim:]
    return jnp.concatenate([first_half * cosine - second_half * sine_part, second_half * cosine + first_half * sine_part], axis=-1)

def reference(tokens, norm_gain, w_qkv, w_out, kv_cache, lengths):
    widened = tokens.astype(jnp.float32)
    squares = lax.optimization_barrier(jnp.sum(widened * widened, axis=1))
    inverse_rms = 1.0 / jnp.sqrt(squares / D + 1e-05)
    normed = (widened * inverse_rms[:, None] * norm_gain.astype(jnp.float32)[None, :]).astype(jnp.bfloat16)
    qkv = jnp.dot(normed, w_qkv, preferred_element_type=jnp.float32).astype(jnp.bfloat16)
    group_size = HQ // KVH
    queries = qkv[:, :HQ * DH].astype(jnp.float32).reshape(ROWS, HQ, DH)
    new_keys = qkv[:, HQ * DH:(HQ + KVH) * DH].astype(jnp.float32).reshape(ROWS, KVH, DH)
    new_values = qkv[:, (HQ + KVH) * DH:].reshape(ROWS, KVH, DH)
    positions = lengths.astype(jnp.float32)[:, None, None]
    queries = lax.optimization_barrier(rotate(queries, positions).astype(jnp.bfloat16))
    new_keys = lax.optimization_barrier(rotate(new_keys, positions).astype(jnp.bfloat16))
    score_scale = 1.0 / math.sqrt(DH)

    def one_row(row_items):
        query_row, key_row, value_row, cached_keys, cached_values, length = row_items
        grouped = query_row.astype(jnp.float32).reshape(KVH, group_size, DH)
        keys_wide = cached_keys.astype(jnp.float32).reshape(L, KVH, DH)
        values_wide = cached_values.astype(jnp.float32).reshape(L, KVH, DH)
        scores = jnp.einsum('gqd,pgd->gqp', grouped, keys_wide) * score_scale
        valid_mask = jnp.arange(L, dtype=jnp.int32) < length
        own_scores = jnp.einsum('gqd,gd->gq', grouped, key_row.astype(jnp.float32)) * score_scale
        top = jnp.maximum(lax.optimization_barrier(jnp.max(jnp.where(valid_mask[None, None, :], scores, -1e+30), axis=-1)), own_scores)
        probs = jnp.where(valid_mask[None, None, :], jnp.exp(scores - top[..., None]), 0.0)
        own_probs = jnp.exp(own_scores - top)
        totals = lax.optimization_barrier(jnp.sum(probs, axis=-1)) + own_probs
        rounded = lax.optimization_barrier(probs.astype(jnp.bfloat16)).astype(jnp.float32)
        own_rounded = lax.optimization_barrier(own_probs.astype(jnp.bfloat16)).astype(jnp.float32)
        weighted = jnp.einsum('gqp,pgd->gqd', rounded, values_wide)
        weighted = weighted + own_rounded[..., None] * value_row.astype(jnp.float32)[:, None, :]
        return (weighted / totals[..., None]).reshape(HQ * DH).astype(jnp.bfloat16)
    attention = lax.map(one_row, (queries, new_keys, new_values, kv_cache[0], kv_cache[1], lengths))
    return jnp.dot(attention, w_out, preferred_element_type=jnp.float32).astype(jnp.bfloat16)
```

```python
import functools
import math

import jax
import jax.numpy as jnp
import numpy as np
from jax import lax
from jax.experimental import pallas as pl
from jax.experimental.pallas import tpu as pltpu
from jax.sharding import PartitionSpec as P

HQ = 64
KVH = 4
DH = 128
GROUP = HQ // KVH
EPS = 1e-05
LOWEST = -1e30
FLOOR = -1e29
EXP2_SCALE = math.log2(math.e) / math.sqrt(DH)
ROWS_AXES = ("width", "sub")
F32 = jnp.float32
BF16 = jnp.bfloat16
VMEM = pl.BlockSpec(memory_space=pltpu.VMEM)
SMEM = pl.BlockSpec(memory_space=pltpu.SMEM)


def three_parts(value):
    high = value.astype(BF16).astype(F32)
    rest = value - high
    middle = rest.astype(BF16).astype(F32)
    return high, middle, rest - middle


def exchange(pieces, axes, count):
    return [pieces[0]] + [
        lax.ppermute(pieces[j], axes, [(i, i ^ j) for i in range(count)])
        for j in range(1, count)
    ]


def column_tile(columns):
    return 256 if columns % 256 == 0 else columns


def rope_kernel(lengths_ref, frequency_ref, cosine_ref, sine_ref):
    rows = cosine_ref.shape[0]
    row = lax.broadcasted_iota(jnp.int32, (rows, DH), 0)
    lane = lax.broadcasted_iota(jnp.int32, (rows, DH), 1)
    position = jnp.zeros((rows, DH), jnp.int32)
    for r in range(rows):
        position = jnp.where(row == r, lengths_ref[r], position)
    angle = position.astype(F32) * frequency_ref[...]
    sine = jnp.sin(angle)
    cosine_ref[...] = jnp.cos(angle)
    sine_ref[...] = jnp.where(lane < DH // 2, -sine, sine)


def project_kernel(n_f, n_w, *refs):
    slots, (gain_ref, w_ref), outs = refs[:n_f], refs[n_f : n_f + 2], refs[n_f + 2 : n_f + 2 + n_w]
    lhs, result = refs[n_f + 2 + n_w :]
    rows = slots[0].shape[0]
    total = n_f * rows
    columns = w_ref.shape[1]
    widened = jnp.concatenate([slot[...].astype(F32) for slot in slots], axis=0)
    squares = jnp.sum(widened * widened, axis=1, keepdims=True)
    scaled = widened * gain_ref[...].astype(F32)
    high = scaled.astype(BF16)
    lhs[:total] = high
    lhs[total:] = (scaled - high.astype(F32)).astype(BF16)
    lane = lax.broadcasted_iota(jnp.int32, (total, 128), 1)
    stats = jnp.zeros((total, 128), F32)
    for at, part in enumerate(three_parts(squares)):
        stats = jnp.where(lane == at, part, stats)
    for k in range(n_f):
        result[k, :, :128] = stats[k * rows : (k + 1) * rows]
    tile = column_tile(columns)

    def step(at, carry):
        start = at * tile
        product = jnp.dot(lhs[...], w_ref[:, pl.ds(pl.multiple_of(start, tile), tile)], preferred_element_type=F32)
        product = product[:total] + product[total:]
        where = pl.ds(pl.multiple_of(start + 128, 128), tile)
        for k in range(n_f):
            result[k, :, where] = product[k * rows : (k + 1) * rows]
        return carry

    if columns == tile:
        product = jnp.dot(lhs[...], w_ref[...], preferred_element_type=F32)
        product = product[:total] + product[total:]
        for k in range(n_f):
            result[k, :, 128:] = product[k * rows : (k + 1) * rows]
    else:
        lax.fori_loop(0, columns // tile, step, 0)
    mine = jnp.bitwise_xor(lax.axis_index("ffn"), lax.axis_index(ROWS_AXES))
    for j in range(n_w):
        outs[j][...] = result[jnp.bitwise_xor(mine, j)].astype(BF16)


def normalise_kernel(features, *refs):
    parts, out = refs[:-1], refs[-1]
    total = parts[0][...].astype(F32)
    for part in parts[1:]:
        total = total + part[...].astype(F32)
    squares = jnp.sum(total[:, :128], axis=1, keepdims=True)
    inverse_rms = 1.0 / jnp.sqrt(squares / features + EPS)
    out[...] = (total[:, 128:] * inverse_rms).astype(BF16)


def attend_kernel(n_f, *refs):
    slots = refs[:n_f]
    cosine_ref, sine_ref, lengths_ref, cache_ref = refs[n_f : n_f + 4]
    outs = refs[n_f + 4 : 2 * n_f + 4]
    shards, heads, results = refs[2 * n_f + 4 :]
    rows, columns = slots[0].shape
    block = cache_ref.shape[2]
    per = HQ // n_f
    f = lax.axis_index("ffn")
    for k in range(n_f):
        shards[jnp.bitwise_xor(f, k)] = slots[k][...].astype(F32)
    for h in range(HQ + 2 * KVH):
        at, end, found = h * DH, (h + 1) * DH, []
        while at < end:
            b, offset = divmod(at, columns)
            length = min(end - at, columns - offset)
            found.append(shards[b, :, offset : offset + length])
            at += length
        heads[:, h, :] = found[0] if len(found) == 1 else jnp.concatenate(found, axis=1)
    lane = lax.broadcasted_iota(jnp.int32, (HQ, 128), 1)
    stats = jnp.zeros((HQ, 128), F32)
    position = f * block + lax.broadcasted_iota(jnp.int32, (1, block), 1)
    for r in range(rows):
        turn_c, turn_s = cosine_ref[r : r + 1, :], sine_ref[r : r + 1, :]

        def rotate(values):
            return (values * turn_c + pltpu.roll(values, DH // 2, 1) * turn_s).astype(BF16)

        queries = rotate(heads[r, :HQ, :])
        joined = heads[r, HQ:, :]
        new_keys = rotate(joined).astype(F32)
        new_values = joined[KVH:]
        empty = jnp.zeros((GROUP, DH), BF16)
        spread = jnp.concatenate(
            [
                jnp.concatenate(
                    [queries[g * GROUP : (g + 1) * GROUP] if c == g else empty for c in range(KVH)], axis=1
                )
                for g in range(KVH)
            ],
            axis=0,
        )
        scores = lax.dot_general(
            spread, cache_ref[0, r], (((1,), (1,)), ((), ())), preferred_element_type=F32
        )
        scores = jnp.where(position < lengths_ref[r], scores, LOWEST)
        keys_wide = jnp.concatenate(
            [jnp.broadcast_to(new_keys[g : g + 1], (GROUP, DH)) for g in range(KVH)], axis=0
        )
        values_wide = jnp.concatenate(
            [jnp.broadcast_to(new_values[g : g + 1], (GROUP, DH)) for g in range(KVH)], axis=0
        )
        own = jnp.sum(queries.astype(F32) * keys_wide, axis=1, keepdims=True)
        own = jnp.where(f == 0, own, LOWEST)
        top = jnp.maximum(jnp.maximum(jnp.max(scores, axis=1, keepdims=True), own), FLOOR)
        probs = jnp.exp2((scores - top) * EXP2_SCALE)
        own_probs = jnp.exp2((own - top) * EXP2_SCALE)
        totals = jnp.sum(probs, axis=1, keepdims=True) + own_probs
        weighted = jnp.dot(probs.astype(BF16), cache_ref[1, r], preferred_element_type=F32)
        weighted = jnp.concatenate(
            [weighted[g * GROUP : (g + 1) * GROUP, g * DH : (g + 1) * DH] for g in range(KVH)], axis=0
        )
        weighted = weighted + own_probs.astype(BF16).astype(F32) * values_wide
        for b in range(n_f):
            results[b, r] = weighted[b * per : (b + 1) * per]
        for at, part in enumerate(three_parts(top) + three_parts(totals)):
            stats = jnp.where(lane == 8 * r + at, part, stats)
    for b in range(n_f):
        results[b, rows] = stats[b * per : (b + 1) * per]
    for j in range(n_f):
        outs[j][...] = results[jnp.bitwise_xor(f, j)].astype(BF16)


def combine_kernel(*refs):
    parts, out = refs[:-1], refs[-1]
    rows = out.shape[0]
    for r in range(rows):
        tops, totals = [], []
        for part in parts:
            stats = part[rows].astype(F32)
            at = 8 * r
            tops.append(stats[:, at : at + 1] + stats[:, at + 1 : at + 2] + stats[:, at + 2 : at + 3])
            totals.append(stats[:, at + 3 : at + 4] + stats[:, at + 4 : at + 5] + stats[:, at + 5 : at + 6])
        top = functools.reduce(jnp.maximum, tops)
        weighted, total = 0.0, 0.0
        for k, part in enumerate(parts):
            share = jnp.exp2((tops[k] - top) * EXP2_SCALE)
            weighted = weighted + share * part[r].astype(F32)
            total = total + share * totals[k]
        out[r] = (weighted / total).astype(BF16)


def output_kernel(n_f, n_w, *refs):
    slots, w_ref, outs = refs[:n_w], refs[n_w], refs[n_w + 1 : n_w + 1 + n_f]
    wide, lhs, result = refs[n_w + 1 + n_f :]
    rows, per, _ = slots[0].shape
    columns = w_ref.shape[1]
    for j in range(n_w):
        wide[j * rows : (j + 1) * rows] = slots[j][...].astype(F32)
    for h in range(per):
        lhs[:, h * DH : (h + 1) * DH] = wide[:, h, :].astype(BF16)
    tile = column_tile(columns)

    def step(at, carry):
        where = pl.ds(pl.multiple_of(at * tile, tile), tile)
        product = jnp.dot(lhs[...], w_ref[:, where], preferred_element_type=F32)
        for j in range(n_w):
            result[j, :, where] = product[j * rows : (j + 1) * rows]
        return carry

    lax.fori_loop(0, columns // tile, step, 0)
    mine = jnp.bitwise_xor(lax.axis_index("ffn"), lax.axis_index(ROWS_AXES))
    for j in range(n_f):
        outs[j][...] = result[jnp.bitwise_xor(mine, j)].astype(BF16)


def sum_kernel(*refs):
    total = refs[0][...].astype(F32)
    for part in refs[1:-1]:
        total = total + part[...].astype(F32)
    refs[-1][...] = total.astype(BF16)


def call(kernel, outs, inputs, name, scratch=(), smem=(), limit=4):
    many = isinstance(outs, list)
    return pl.pallas_call(
        kernel,
        out_shape=outs,
        in_specs=[SMEM if at in smem else VMEM for at in range(len(inputs))],
        out_specs=[VMEM] * len(outs) if many else VMEM,
        scratch_shapes=list(scratch),
        compiler_params=pltpu.CompilerParams(vmem_limit_bytes=limit << 20),
        name=name,
    )(*inputs)


def local(n_f, n_w, tokens, norm_gain, w_qkv, w_out, kv_cache, lengths):
    rows, features = tokens.shape
    columns, out_columns = w_qkv.shape[1], w_out.shape[1]
    per = HQ // n_f
    shape = jax.ShapeDtypeStruct
    w_qkv = pltpu.with_memory_space_constraint(w_qkv, pltpu.VMEM)
    w_out = pltpu.with_memory_space_constraint(w_out, pltpu.VMEM)
    kv_cache = pltpu.with_memory_space_constraint(kv_cache, pltpu.VMEM)
    half = 500000.0 ** (-(np.arange(DH // 2, dtype=np.float64) * 2.0 / DH))
    frequency = jnp.asarray(np.concatenate([half, half])[None, :], F32)

    token_slots = exchange([tokens] * n_f, "ffn", n_f)
    cosine, sine = call(
        rope_kernel, [shape((rows, DH), F32)] * 2, [lengths, frequency], "rope", smem=(0,)
    )
    projected = call(
        functools.partial(project_kernel, n_f, n_w),
        [shape((rows, 128 + columns), BF16)] * n_w,
        token_slots + [norm_gain.reshape(1, features), w_qkv],
        "project",
        scratch=[
            pltpu.VMEM((2 * n_f * rows, features), BF16),
            pltpu.VMEM((n_f, rows, 128 + columns), F32),
        ],
    )
    partials = exchange(projected, ROWS_AXES, n_w)
    qkv = call(
        functools.partial(normalise_kernel, float(features * n_w)),
        shape((rows, columns), BF16),
        partials,
        "normalise",
    )
    qkv_slots = exchange([qkv] * n_f, "ffn", n_f)
    attended = call(
        functools.partial(attend_kernel, n_f),
        [shape((rows + 1, per, DH), BF16)] * n_f,
        qkv_slots + [cosine, sine, lengths, kv_cache],
        "attend",
        scratch=[
            pltpu.VMEM((n_f, rows, columns), F32),
            pltpu.VMEM((rows, HQ + 2 * KVH, DH), F32),
            pltpu.VMEM((n_f, rows + 1, per, DH), F32),
        ],
        smem=(n_f + 2,),
    )
    attention = call(
        combine_kernel,
        shape((rows, per, DH), BF16),
        exchange(attended, "ffn", n_f),
        "combine",
    )
    row_slots = exchange([attention] * n_w, ROWS_AXES, n_w)
    summands = call(
        functools.partial(output_kernel, n_f, n_w),
        [shape((rows, out_columns), BF16)] * n_f,
        row_slots + [w_out],
        "output",
        scratch=[
            pltpu.VMEM((n_w * rows, per, DH), F32),
            pltpu.VMEM((n_w * rows, per * DH), BF16),
            pltpu.VMEM((n_w, rows, out_columns), F32),
        ],
    )
    return call(
        sum_kernel, shape((rows, out_columns), BF16), exchange(summands, "ffn", n_f), "total"
    )


def solution(mesh):
    placed = (
        P(("groups", "ffn"), ("width", "sub")),
        P(("width", "sub")),
        P(("width", "sub"), "ffn"),
        P("ffn", ("width", "sub")),
        P(None, ("groups", "width", "sub"), "ffn", None),
        P(("groups", "width", "sub")),
    )
    n_f, n_w = mesh.shape["ffn"], mesh.shape["width"] * mesh.shape["sub"]
    assert n_f == n_w and n_f & (n_f - 1) == 0
    return jax.shard_map(
        functools.partial(local, n_f, n_w),
        mesh=mesh,
        in_specs=placed,
        out_specs=P(("groups", "ffn"), ("width", "sub")),
        check_vma=False,
    )
```

```python
import functools
import math

import jax
import jax.numpy as jnp
import numpy as np
from jax import lax
from jax.experimental import pallas as pl
from jax.experimental.pallas import tpu as pltpu
from jax.sharding import PartitionSpec as P

HQ = 64
KVH = 4
DH = 128
GROUP = HQ // KVH
EPS = 1e-05
LOWEST = -1e30
FLOOR = -1e29
EXP2_SCALE = math.log2(math.e) / math.sqrt(DH)
ROWS_AXES = ("width", "sub")
F32 = jnp.float32
BF16 = jnp.bfloat16
VMEM = pl.BlockSpec(memory_space=pltpu.VMEM)
SMEM = pl.BlockSpec(memory_space=pltpu.SMEM)


def three_parts(value):
    high = value.astype(BF16).astype(F32)
    rest = value - high
    middle = rest.astype(BF16).astype(F32)
    return high, middle, rest - middle


def exchange(pieces, axes, count):
    arrived = [pieces[0]] * count
    for j in range(count - 1, 0, -1):
        arrived[j] = lax.ppermute(pieces[j], axes, [(i, i ^ j) for i in range(count)])
    return arrived


def prelude_kernel(first_ref):
    first_ref[...] = jnp.zeros_like(first_ref)


def rope_kernel(lengths_ref, frequency_ref, cosine_ref, sine_ref):
    rows = cosine_ref.shape[0]
    row = lax.broadcasted_iota(jnp.int32, (rows, DH), 0)
    lane = lax.broadcasted_iota(jnp.int32, (rows, DH), 1)
    position = jnp.zeros((rows, DH), jnp.int32)
    for r in range(rows):
        position = jnp.where(row == r, lengths_ref[r], position)
    angle = position.astype(F32) * frequency_ref[...]
    sine = jnp.sin(angle)
    cosine_ref[...] = jnp.cos(angle)
    sine_ref[...] = jnp.where(lane < DH // 2, -sine, sine)


def project_kernel(order, n_w, *refs):
    n_f = len(order)
    slots, (gain_ref, w_ref, _), outs = refs[:n_f], refs[n_f : n_f + 3], refs[n_f + 3 : n_f + 3 + n_w]
    lhs, result = refs[n_f + 3 + n_w :]
    rows = slots[0].shape[0]
    total = n_f * rows
    columns = w_ref.shape[1]
    widened = jnp.concatenate([slot[...].astype(F32) for slot in slots], axis=0)
    squares = jnp.sum(widened * widened, axis=1, keepdims=True)
    scaled = widened * gain_ref[...].astype(F32).reshape(1, -1)
    lhs[...] = scaled.astype(BF16)
    lane = lax.broadcasted_iota(jnp.int32, (total, 128), 1)
    stats = jnp.zeros((total, 128), F32)
    for at, part in enumerate(three_parts(squares)):
        stats = jnp.where(lane == at, part, stats)
    for k in range(n_f):
        result[order[k], :, :128] = stats[k * rows : (k + 1) * rows]
    product = jnp.dot(lhs[...], w_ref[...], preferred_element_type=F32)
    for k in range(n_f):
        result[order[k], :, 128:] = product[k * rows : (k + 1) * rows]
    mine = jnp.bitwise_xor(lax.axis_index("ffn"), lax.axis_index(ROWS_AXES))
    for j in range(n_w):
        outs[-1 - j][...] = result[jnp.bitwise_xor(mine, j)].astype(BF16)


def normalise_kernel(features, *refs):
    parts, out = refs[:-1], refs[-1]
    total = parts[0][...].astype(F32)
    for part in parts[1:]:
        total = total + part[...].astype(F32)
    squares = jnp.sum(total[:, :128], axis=1, keepdims=True)
    inverse_rms = 1.0 / jnp.sqrt(squares / features + EPS)
    out[...] = (total[:, 128:] * inverse_rms).astype(BF16)


def prepare(n_f, f, slots, cosine_ref, sine_ref, shards, heads, queries_ref, own_ref):
    rows, columns = slots[0].shape
    per = HQ // n_f
    for k in range(n_f):
        shards[jnp.bitwise_xor(f, k)] = slots[k][...].astype(F32)
    for h in range(HQ + 2 * KVH):
        at, end, found = h * DH, (h + 1) * DH, []
        while at < end:
            b, offset = divmod(at, columns)
            length = min(end - at, columns - offset)
            found.append(shards[b, :, offset : offset + length])
            at += length
        heads[:, h, :] = found[0] if len(found) == 1 else jnp.concatenate(found, axis=1)
    for r in range(rows):
        values = heads[r]
        turned = values * cosine_ref[r : r + 1, :] + pltpu.roll(values, DH // 2, 1) * sine_ref[r : r + 1, :]
        for b in range(n_f):
            queries_ref[b, r] = turned[b * per : (b + 1) * per].astype(BF16)
        new_keys = turned[HQ : HQ + KVH].astype(BF16).astype(F32)
        for g in range(KVH):
            own_ref[0, g, r : r + 1] = new_keys[g : g + 1]
            own_ref[1, g, r : r + 1] = values[HQ + KVH + g : HQ + KVH + g + 1]


def turn_keys_kernel(cache_ref, _, keys_ref):
    for r in range(keys_ref.shape[0]):
        keys_ref[r] = cache_ref[0, r].T


def attend(f, peers, queries_ref, own_ref, lengths_ref, keys_ref, cache_ref, outs, scores, probs):
    rows, per = queries_ref.shape[1:3]
    block = cache_ref.shape[2]
    position = f * block + lax.broadcasted_iota(jnp.int32, (1, block), 1)
    lane = lax.broadcasted_iota(jnp.int32, (per, 128), 1)
    theirs = [jnp.bitwise_xor(f, j) for j in peers]
    groups = [lax.div(b * per, GROUP) for b in theirs]
    for r in range(rows):
        for n, (b, g) in enumerate(zip(theirs, groups)):
            keys = keys_ref[r, pl.ds(pl.multiple_of(g * DH, DH), DH), :]
            scores[n, r] = jnp.dot(queries_ref[b, r], keys, preferred_element_type=F32)
    added, stats = {}, [jnp.zeros((per, 128), F32) for _ in peers]
    for r in range(rows):
        for n, (b, g) in enumerate(zip(theirs, groups)):
            raw = jnp.where(position < lengths_ref[r], scores[n, r], LOWEST)
            own = jnp.sum(queries_ref[b, r].astype(F32) * own_ref[0, g, r : r + 1], axis=1, keepdims=True)
            own = jnp.where(f == 0, own, LOWEST)
            top = jnp.maximum(jnp.maximum(jnp.max(raw, axis=1, keepdims=True), own), FLOOR)
            chances = jnp.exp2((raw - top) * EXP2_SCALE)
            own_chance = jnp.exp2((own - top) * EXP2_SCALE)
            totals = jnp.sum(chances, axis=1, keepdims=True) + own_chance
            probs[n, r] = chances.astype(BF16)
            added[n, r] = own_chance.astype(BF16).astype(F32) * own_ref[1, g, r : r + 1]
            for at, part in enumerate(three_parts(top) + three_parts(totals)):
                stats[n] = jnp.where(lane == 8 * r + at, part, stats[n])
    for r in range(rows):
        for n, g in enumerate(groups):
            values = cache_ref[1, r, :, pl.ds(pl.multiple_of(g * DH, DH), DH)]
            weighted = jnp.dot(probs[n, r], values, preferred_element_type=F32) + added[n, r]
            outs[n][r] = weighted.astype(BF16)
    for n in range(len(peers)):
        outs[n][rows] = stats[n].astype(BF16)


def attend_first_kernel(n_f, peers, *refs):
    slots = refs[:n_f]
    cosine_ref, sine_ref, lengths_ref, keys_ref, cache_ref, queries_ref, own_ref = refs[n_f : n_f + 7]
    outs, (shards, heads, scores, probs) = refs[n_f + 7 : -4], refs[-4:]
    f = lax.axis_index("ffn")
    prepare(n_f, f, slots, cosine_ref, sine_ref, shards, heads, queries_ref, own_ref)
    attend(f, peers, queries_ref, own_ref, lengths_ref, keys_ref, cache_ref, outs, scores, probs)


def attend_more_kernel(peers, queries_ref, own_ref, lengths_ref, keys_ref, cache_ref, *refs):
    attend(
        lax.axis_index("ffn"),
        peers,
        queries_ref,
        own_ref,
        lengths_ref,
        keys_ref,
        cache_ref,
        refs[:-2],
        *refs[-2:],
    )


def combine_kernel(*refs):
    parts, out = refs[:-1], refs[-1]
    rows = out.shape[0]

    def lane_sum(values, first):
        return sum(
            pltpu.roll(values, (128 - at) % 128, 1) if at else values for at in range(first, first + 3)
        )

    stats = [part[rows].astype(F32) for part in parts]
    tops = [lane_sum(values, 0) for values in stats]
    top = functools.reduce(jnp.maximum, tops)
    shares = [jnp.exp2((one - top) * EXP2_SCALE) for one in tops]
    total = sum(share * lane_sum(values, 3) for share, values in zip(shares, stats))
    for r in range(rows):
        at = slice(8 * r, 8 * r + 1)
        weighted = sum(share[:, at] * part[r].astype(F32) for share, part in zip(shares, parts))
        out[r] = (weighted / total[:, at]).astype(BF16)


def output_kernel(n_f, n_w, *refs):
    slots, w_ref, outs = refs[:n_w], refs[n_w], refs[n_w + 1 : n_w + 1 + n_f]
    wide, lhs, result = refs[n_w + 1 + n_f :]
    rows, per, _ = slots[0].shape
    columns = w_ref.shape[1]
    for j in range(n_w):
        wide[j * rows : (j + 1) * rows] = slots[j][...].astype(F32)
    for h in range(per):
        lhs[:, h * DH : (h + 1) * DH] = wide[:, h, :].astype(BF16)
    product = jnp.dot(lhs[...], w_ref[...], preferred_element_type=F32)
    for j in range(n_w):
        result[j] = product[j * rows : (j + 1) * rows]
    mine = jnp.bitwise_xor(lax.axis_index("ffn"), lax.axis_index(ROWS_AXES))
    for j in range(n_f):
        outs[-1 - j][...] = result[jnp.bitwise_xor(mine, j)].astype(BF16)


def sum_kernel(*refs):
    total = refs[0][...].astype(F32)
    for part in refs[1:-1]:
        total = total + part[...].astype(F32)
    refs[-1][...] = total.astype(BF16)


def call(kernel, outs, inputs, name, micros, scratch=(), smem=(), limit=4):
    many = isinstance(outs, list)
    return pl.pallas_call(
        kernel,
        out_shape=outs,
        in_specs=[SMEM if at in smem else VMEM for at in range(len(inputs))],
        out_specs=[VMEM] * len(outs) if many else VMEM,
        scratch_shapes=list(scratch),
        compiler_params=pltpu.CompilerParams(vmem_limit_bytes=limit << 20),
        cost_estimate=pl.CostEstimate(flops=int(micros * 1e9), bytes_accessed=0, transcendentals=0),
        name=name,
    )(*inputs)


def local(n_f, n_w, tokens, norm_gain, w_qkv, w_out, kv_cache, lengths):
    rows, features = tokens.shape
    columns, out_columns = w_qkv.shape[1], w_out.shape[1]
    per = HQ // n_f
    shape = jax.ShapeDtypeStruct
    w_qkv = pltpu.with_memory_space_constraint(w_qkv, pltpu.VMEM)
    w_out = pltpu.with_memory_space_constraint(w_out, pltpu.VMEM)
    kv_cache = pltpu.with_memory_space_constraint(kv_cache, pltpu.VMEM)
    half = 500000.0 ** (-(np.arange(DH // 2, dtype=np.float64) * 2.0 / DH))
    frequency = jnp.asarray(np.concatenate([half, half])[None, :], F32)

    token_slots = exchange([tokens] * n_f, "ffn", n_f)
    order = [0] + list(range(n_f - 1, 0, -1))
    first = call(prelude_kernel, shape((8, 128), F32), [], "prelude", 40)
    cosine, sine = call(
        rope_kernel, [shape((rows, DH), F32)] * 2, [lengths, frequency], "rope", 5, smem=(0,)
    )
    projected = call(
        functools.partial(project_kernel, order, n_w),
        [shape((rows, 128 + columns), BF16)] * n_w,
        [token_slots[k] for k in order] + [norm_gain, w_qkv, first],
        "project",
        20,
        scratch=[
            pltpu.VMEM((n_f * rows, features), BF16),
            pltpu.VMEM((n_f, rows, 128 + columns), F32),
        ],
    )
    partials = exchange(projected[::-1], ROWS_AXES, n_w)[::-1]
    qkv = call(
        functools.partial(normalise_kernel, float(features * n_w)),
        shape((rows, columns), BF16),
        partials,
        "normalise",
        10,
    )
    qkv_slots = exchange([qkv] * n_f, "ffn", n_f)
    keys = call(
        turn_keys_kernel,
        shape((rows, kv_cache.shape[3], kv_cache.shape[2]), BF16),
        [kv_cache, qkv],
        "turn_keys",
        5,
    )
    waves = [list(range(n_f - 1, 0, -1)), [0]]
    piece = shape((rows + 1, per, DH), BF16)
    room = [
        [pltpu.VMEM((len(peers), rows, per, kv_cache.shape[2]), kind) for kind in (F32, BF16)]
        for peers in waves
    ]
    queries, own, *found = call(
        functools.partial(attend_first_kernel, n_f, waves[0]),
        [shape((n_f, rows, per, DH), BF16), shape((2, KVH, rows, DH), F32)] + [piece] * len(waves[0]),
        qkv_slots + [cosine, sine, lengths, keys, kv_cache],
        "attend_first",
        20,
        scratch=[
            pltpu.VMEM((n_f, rows, columns), F32),
            pltpu.VMEM((rows, HQ + 2 * KVH, DH), F32),
        ]
        + room[0],
        smem=(n_f + 2,),
        limit=8,
    )
    attended = dict(zip(waves[0], found))
    for peers, rooms in zip(waves[1:], room[1:]):
        found = call(
            functools.partial(attend_more_kernel, peers),
            [piece] * len(peers),
            [queries, own, lengths, keys, kv_cache],
            "attend_more",
            5,
            scratch=rooms,
            smem=(2,),
        )
        attended.update(zip(peers, found))
    attended = [attended[j] for j in range(n_f)]
    attention = call(
        combine_kernel,
        shape((rows, per, DH), BF16),
        exchange(attended, "ffn", n_f)[::-1],
        "combine",
        10,
    )
    row_slots = exchange([attention] * n_w, ROWS_AXES, n_w)
    summands = call(
        functools.partial(output_kernel, n_f, n_w),
        [shape((rows, out_columns), BF16)] * n_f,
        row_slots + [w_out],
        "output",
        10,
        scratch=[
            pltpu.VMEM((n_w * rows, per, DH), F32),
            pltpu.VMEM((n_w * rows, per * DH), BF16),
            pltpu.VMEM((n_w, rows, out_columns), F32),
        ],
    )
    return call(
        sum_kernel, shape((rows, out_columns), BF16), exchange(summands[::-1], "ffn", n_f)[::-1], "total", 1
    )


def solution(mesh):
    placed = (
        P(("groups", "ffn"), ("width", "sub")),
        P(("width", "sub")),
        P(("width", "sub"), "ffn"),
        P("ffn", ("width", "sub")),
        P(None, ("groups", "width", "sub"), "ffn", None),
        P(("groups", "width", "sub")),
    )
    n_f, n_w = mesh.shape["ffn"], mesh.shape["width"] * mesh.shape["sub"]
    assert n_f == n_w and n_f & (n_f - 1) == 0
    return jax.shard_map(
        functools.partial(local, n_f, n_w),
        mesh=mesh,
        in_specs=placed,
        out_specs=P(("groups", "ffn"), ("width", "sub")),
        check_vma=False,
    )
```
